32 devices in a mesh: pair: 16 (over z, y, x), vir: 2 (over core).
Axes of the slice: x: 2, y: 2, z: 4, core: 2. Of those that a mesh axis runs over, the one named last changes fastest.
Arguments:
- amplitudes: bfloat16 [40960, 1024], P('pair', 'vir'), may hold values from -6 to 6
- cycle_ints: bfloat16 [40960, 1024], P('pair', 'vir'), may hold values from -6 to 6
- int_rows: bfloat16 [1024, 1024], P('pair', 'vir'), may hold values from -6 to 6
- row_dest: int32 [1024, 2], P('pair'), may hold values from 0 to 15, all different within a row; in each aligned block of 64 rows (0 to 63, 64 to 127, ...) at most 16 rows name the same one
- vir_energy: float32 [1024], P('vir'), may hold values from 0.5 to 4
- occ_energy: float32 [40960], P('pair'), may hold values from -2 to -0.2
Outputs:
- residual: bfloat16 [40960, 1024], P('pair', 'vir')
The draws below stay inside these ranges and needn't reach their ends.
Inputs may be any that keep to these rules, and one draw needn't show every extreme that they name: `row_dest`: each integral row names 2 different pair groups; among the 64 rows of one pair group no group is named more than 16 times, a bound that some block reaches.
All inputs are finite; a program needn't handle non-finite values.
Results may differ from the reference program's by a relative error of at most 0.008.
Values may be sent and summed in bfloat16 or wider, within the bound.
A program may use at most 64 MiB of HBM per device.

```python
import math
import jax
import jax.numpy as jnp
import numpy as np
from jax import lax

NV = 1024
ROWS = 2560
R_DEV = 64
TOP = 2
SLOTS = 256
NPR = 40960
NR = 1024
N_PAIR = 16


def steps_of(rng, shape, cuts, least, high):
    factor_of, own = 1.0, jax.random.fold_in(rng, 6)
    for axis_at, shards_of in cuts:
        heights = jnp.exp(jax.random.uniform(jax.random.fold_in(own, axis_at), (shards_of,), jnp.float32, least / len(cuts), high / len(cuts)))
        factor_of = factor_of * jnp.repeat(heights, shape[axis_at] // shards_of).reshape([-1 if axis == axis_at else 1 for axis in range(len(shape))])
    return factor_of


def shared_out(own_key, own, number, rows, number_of, top, most, slope):
    order = jax.random.permutation(own_key, number_of)
    crowded, ordinary = load_shares(number_of, rows * top, most, slope, True), load_shares(number_of, rows * top, most, slope, False)
    places = jnp.arange(number_of)

    def named(sizes, rotation):
        used = int((sizes > 0).sum())
        fixed = max(1, used // 4)
        passed = fixed + (places - fixed + rotation * (used - fixed)) % max(1, number_of - fixed)
        return jnp.zeros((number_of,), jnp.int32).at[order[jnp.where(places < fixed, places, passed)]].set(jnp.asarray(sizes, jnp.int32))

    sizes = jnp.where(number % 4 == 0, named(crowded, number // 4), named(ordinary, number - number // 4 - 1))
    mixed = jax.random.permutation(jax.random.fold_in(own, 3), number_of)
    giver, receiver = mixed[0:number_of // 2 * 2:2], mixed[1:number_of // 2 * 2:2]
    room = jnp.minimum(sizes[giver] - 1, most - sizes[receiver]) // 2
    room = jnp.where((giver == order[0]) | (receiver == order[0]) | (sizes[receiver] == 0), 0, jnp.maximum(room, 0))
    passed = jax.random.randint(jax.random.fold_in(own, 4), (number_of // 2,), 0, 1 << 20) % (room + 1)
    sizes = sizes.at[giver].add(-passed).at[receiver].add(passed)
    labels = jnp.searchsorted(jnp.cumsum(sizes), jnp.arange(rows * top), side="right").astype(jnp.int32)
    grid = labels.reshape(top, rows).T
    grid = grid[jax.random.permutation(jax.random.fold_in(own, 1), rows)]
    rotation = jax.random.randint(jax.random.fold_in(own, 2), (rows, 1), 0, top)
    return jnp.take_along_axis(grid, (jnp.arange(top)[None, :] + rotation) % top, axis=1)


def load_shares(count, total, most, slope, full):
    weights = [(1 << 20) // math.isqrt(grade ** slope) + 1 for grade in range(1, count + 1)]
    largest = most if full else min(most, max(-(-total // count), total * weights[0] // sum(weights)))
    least = 1 if total - largest >= count - 1 else 0
    holding, spare = [largest] + [least] * (count - 1), total - largest - least * (count - 1)
    while spare > 0:
        candidates = [i for i in range(1, count) if holding[i] < largest] or [i for i in range(1, count) if holding[i] < most]
        mass, left = sum([weights[i] for i in candidates]), spare
        for i in candidates:
            more = min(most - holding[i], max(1, left * weights[i] // mass), spare)
            holding[i] = holding[i] + more
            spare = spare - more
    return np.array(holding)


def gaussian(rng, extent, width, limit, cuts=(), held_as=jnp.bfloat16):
    values = width * jax.random.normal(rng, extent, jnp.float32)
    if cuts:
        values = values * steps_of(rng, extent, cuts, -0.22, 0.18)
    return jnp.clip(values, -limit, limit).astype(held_as)


def setup_inputs(seed: int = 0) -> dict:
    splits = jax.random.split(jax.random.key(seed), 7)
    amplitudes = gaussian(splits[0], (NPR, NV), 1.0, 6.0, ((0, 16), (1, 2)))
    cycle_ints = gaussian(splits[1], (NPR, NV), 1.0, 6.0, ((0, 16), (1, 2)))
    int_rows = gaussian(splits[2], (NR, NV), 1.0, 6.0, ((0, 16), (1, 2)))
    row_dest_keys = jax.random.split(jax.random.fold_in(splits[3], 1), NR // R_DEV)
    row_dest_turns = jax.random.permutation(jax.random.fold_in(splits[3], 3), NR // R_DEV)
    row_dest = jax.vmap(lambda own, number: shared_out(jax.random.fold_in(splits[3], 2), own, number, R_DEV, N_PAIR, TOP, SLOTS // N_PAIR, 2))(row_dest_keys, row_dest_turns).reshape((NR, TOP))
    vir_energy = jnp.clip(jnp.exp(math.log(4.0) - 2.0794415 * jax.random.uniform(splits[4], (NV,), jnp.float32) ** steps_of(splits[4], (NV,), ((0, 2),), -0.2, 0.2)), 0.5, 4.0)
    occ_energy = jnp.clip(-2.0 + 1.8 * jax.random.uniform(splits[5], (NPR,), jnp.float32) ** steps_of(splits[5], (NPR,), ((0, 16),), -0.2, 0.2), -2.0, -0.2)
    return {"amplitudes": amplitudes, "cycle_ints": cycle_ints, "int_rows": int_rows, "row_dest": row_dest, "vir_energy": vir_energy, "occ_energy": occ_energy}


def reference(amplitudes, cycle_ints, int_rows, row_dest, vir_energy, occ_energy):
    total_rows = ROWS * N_PAIR
    cross_sum = lax.dot_general(amplitudes, cycle_ints, (((0,), (0,)), ((), ())), preferred_element_type=jnp.float32)
    cross_sum = cross_sum / math.sqrt(total_rows * NV)
    cycle_term = jnp.dot(amplitudes, cross_sum.astype(jnp.bfloat16), preferred_element_type=jnp.float32)
    padded_rows = jnp.concatenate([int_rows, jnp.zeros((1, NV), int_rows.dtype)], axis=0)
    blocks = amplitudes.reshape(N_PAIR, ROWS, NV)

    def ladder_block(group_id):
        amp_block = blocks[group_id]
        routed = jnp.any(row_dest == group_id, axis=1)
        picked = jnp.nonzero(routed, size=SLOTS, fill_value=R_DEV * N_PAIR)[0].astype(jnp.int32)
        chosen = padded_rows[picked]
        coefficient = lax.dot_general(amp_block, chosen, (((1,), (1,)), ((), ())), preferred_element_type=jnp.float32)
        coefficient = coefficient / math.sqrt(NV)
        return jnp.dot(coefficient.astype(jnp.bfloat16), chosen, preferred_element_type=jnp.float32) / math.sqrt(SLOTS)
    ladder = lax.map(ladder_block, jnp.arange(N_PAIR, dtype=jnp.int32)).reshape(total_rows, NV)
    energy = (vir_energy[None, :] - occ_energy[:, None]) * amplitudes.astype(jnp.float32)
    return (cycle_term + ladder + energy).astype(jnp.bfloat16)
```

```python
import math

import jax
import jax.numpy as jnp
from jax import lax
from jax.experimental import pallas as pl
from jax.experimental.pallas import tpu as pltpu
from jax.sharding import PartitionSpec as P

SLOTS = 256


def dispatch(int_rows, row_dest, groups, capacity):
    rows = int_rows.shape[0]
    group = jnp.arange(groups, dtype=jnp.int32)
    member = jnp.any(row_dest[None, :, :] == group[:, None, None], axis=2)
    before = jnp.arange(rows)[:, None] < jnp.arange(rows)[None, :]
    rank = jnp.dot(
        member.astype(jnp.bfloat16), before.astype(jnp.bfloat16), preferred_element_type=jnp.float32
    ).astype(jnp.int32)
    slot = jnp.arange(capacity, dtype=jnp.int32)
    select = member[:, None, :] & (rank[:, None, :] == slot[None, :, None])
    select = select.reshape(groups * capacity, rows).astype(int_rows.dtype)
    return jnp.dot(select, int_rows, preferred_element_type=jnp.float32).astype(int_rows.dtype)


def body(amplitudes, cycle_ints, int_rows, row_dest, vir_energy, occ_energy):
    groups = lax.axis_size("pair")
    row_count, local_width = amplitudes.shape
    full_width = local_width * lax.axis_size("vir")
    capacity = SLOTS // groups
    gathered = lax.all_gather(amplitudes, "vir", axis=1, tiled=True)
    cross_part = lax.dot_general(
        gathered, cycle_ints, (((0,), (0,)), ((), ())), preferred_element_type=jnp.float32
    )
    scale_cycle = math.sqrt(row_count * groups * full_width)
    cross_half = lax.psum((cross_part / scale_cycle).astype(jnp.bfloat16), "pair")
    outgoing = dispatch(int_rows, row_dest, groups, capacity)
    arrived = lax.all_to_all(
        outgoing.reshape(groups, capacity, local_width),
        "pair",
        split_axis=0,
        concat_axis=0,
        tiled=True,
    ).reshape(groups * capacity, local_width)
    chosen = lax.all_gather(arrived, "vir", axis=1, tiled=True)
    coefficient = lax.dot_general(
        gathered, chosen, (((1,), (1,)), ((), ())), preferred_element_type=jnp.float32
    ) / math.sqrt(full_width)
    ladder = jnp.dot(
        coefficient.astype(jnp.bfloat16), arrived, preferred_element_type=jnp.float32
    ) / math.sqrt(SLOTS)
    energy = (vir_energy[None, :] - occ_energy[:, None]) * amplitudes.astype(jnp.float32)
    cycle_term = jnp.dot(gathered, cross_half, preferred_element_type=jnp.float32)
    return (cycle_term + ladder + energy).astype(jnp.bfloat16)


DEPTH, PLANE, UNITS = 4, 4, 4
DIRECT_SUM = ()
DIRECT_SPREAD = (3,)
F32, BF16 = jnp.float32, jnp.bfloat16
MESH = pl.DeviceIdType.MESH


def rows_at(start, size):
    return pl.ds(pl.multiple_of(start, size), size)


def kernel(
    amp_hbm, cyc_hbm, rows_hbm, dest_hbm, vir_hbm, occ_hbm, other, acc, last,
    amp, cyc, rows, dest, vir_e, occ_e, part, first_in, passed, second_in, zsum, z_in, full,
    outgoing, arr, arr_o, gram,
    near_sem, far_sem, load_sem, amp_sem, route_sem, arr_sem, sum_sem, z_sem, gz_sem, spread_sem,
):
    groups = DEPTH * PLANE
    me, v = lax.axis_index("pair"), lax.axis_index("vir")
    z, y, x = me // PLANE, me % PLANE // 2, me % 2
    by_x, by_y, by_xy = me + 1 - 2 * x, me + 2 - 4 * y, z * PLANE + 3 - me % PLANE
    count, width = amp.shape
    full_width = 2 * width
    capacity = SLOTS // groups
    unit = full_width // UNITS
    block = unit // PLANE
    piece = block // DEPTH

    loads = [
        pltpu.make_async_copy(src, dst, load_sem.at[i])
        for i, (src, dst) in enumerate(
            (
                (dest_hbm, dest), (rows_hbm, rows), (amp_hbm, amp), (cyc_hbm, cyc),
                (vir_hbm, vir_e), (occ_hbm, occ_e),
            )
        )
    ]
    barrier = pltpu.get_barrier_semaphore()
    pl.semaphore_signal(barrier, inc=1, device_id=(me, 1 - v), device_id_type=MESH)
    for k in range(1, groups):
        to = (me + k) % groups
        hops = jnp.abs(to // PLANE - z) + jnp.abs(to % PLANE // 2 - y) + jnp.abs(to % 2 - x)
        core = jnp.where(hops == 1, 0, 1)
        pl.semaphore_signal(barrier, inc=1, device_id=(to, core), device_id_type=MESH)
    near = 2 + jnp.where(z > 0, 1, 0) + jnp.where(z < DEPTH - 1, 1, 0)
    for c in loads:
        c.start()

    started = []

    def copy(src, dst, sem, index, device):
        c = pltpu.make_async_remote_copy(
            src_ref=src,
            dst_ref=dst,
            send_sem=sem.at[(0, *index)],
            recv_sem=sem.at[(1, *index)],
            device_id=device,
            device_id_type=MESH,
        )
        c.start()
        started.append(c)
        return c

    loads[0].wait()
    loads[1].wait()
    group = lax.broadcasted_iota(jnp.int32, (SLOTS, rows.shape[0]), 0) // capacity
    slot = lax.broadcasted_iota(jnp.int32, (SLOTS, rows.shape[0]), 0) % capacity
    member = group == dest[0:1, :]
    for k in range(1, dest.shape[0]):
        member = member | (group == dest[k : k + 1, :])
    tri = (rows.shape[0], rows.shape[0])
    before = lax.broadcasted_iota(jnp.int32, tri, 0) < lax.broadcasted_iota(jnp.int32, tri, 1)
    rank = jnp.dot(
        jnp.where(member, 1.0, 0.0).astype(BF16),
        jnp.where(before, 1.0, 0.0).astype(BF16),
        preferred_element_type=F32,
    )
    select = jnp.where(member & (rank == slot.astype(F32)), 1.0, 0.0).astype(BF16)
    outgoing[...] = jnp.dot(select, rows[...], preferred_element_type=F32).astype(BF16)
    mine = rows_at(me * capacity, capacity)
    arr[mine, :] = outgoing[mine, :]

    def cross(u):
        src = amp if u < UNITS // 2 else other
        at = u % (UNITS // 2) * unit
        part[u] = lax.dot_general(
            src[:, at : at + unit], cyc[...], (((0,), (0,)), ((), ())), preferred_element_type=F32
        ).astype(BF16)

    def axes(u):
        return (x, y, by_x, by_y) if u % 2 == 0 else (y, x, by_y, by_x)

    def quarter(a, b):
        return rows_at((a * 2 + b) * block, block)

    sums = {}

    def sum_first(u):
        a, b, by_a, by_b = axes(u)
        if u in DIRECT_SUM:
            sums[u, 0] = copy(
                part.at[u, quarter(1 - a, 1 - b)], first_in.at[u, 0], sum_sem, (u, 0), (by_xy, v)
            )
            sums[u, 2] = copy(
                part.at[u, quarter(a, 1 - b)], second_in.at[u], sum_sem, (u, 2), (by_b, v)
            )
        else:
            sums[u, 0] = copy(
                part.at[u, quarter(1 - a, 1 - b)], first_in.at[u, 0], sum_sem, (u, 0), (by_a, v)
            )
        sums[u, 1] = copy(
            part.at[u, quarter(1 - a, b)], first_in.at[u, 1], sum_sem, (u, 1), (by_a, v)
        )

    def sum_second(u):
        if u in DIRECT_SUM:
            return
        a, b, by_a, by_b = axes(u)
        sums[u, 0].wait_recv()
        passed[u] = (
            part[u, quarter(a, 1 - b), :].astype(F32) + first_in[u, 0].astype(F32)
        ).astype(BF16)
        sums[u, 2] = copy(passed.at[u], second_in.at[u], sum_sem, (u, 2), (by_b, v))

    def sum_third(u):
        a, b, by_a, by_b = axes(u)
        total = part[u, quarter(a, b), :].astype(F32)
        sums[u, 1].wait_recv()
        total += first_in[u, 1].astype(F32)
        if u in DIRECT_SUM:
            sums[u, 0].wait_recv()
            total += first_in[u, 0].astype(F32)
        sums[u, 2].wait_recv()
        zsum[u] = (total + second_in[u].astype(F32)).astype(BF16)
        for e in range(1, DEPTH):
            to = (z + e) % DEPTH
            sums[u, 2 + e] = copy(
                zsum.at[u, rows_at(to * piece, piece)], z_in.at[u, e - 1],
                z_sem, (u, e - 1), (to * PLANE + me % PLANE, v),
            )

    scale = math.sqrt(count * groups * full_width)
    spreads = {}

    def finish(u):
        a, b, by_a, by_b = axes(u)
        total = zsum[u, rows_at(z * piece, piece), :].astype(F32)
        for e in range(1, DEPTH):
            sums[u, 2 + e].wait_recv()
            total += z_in[u, e - 1].astype(F32)
        at = rows_at(((u * 2 + a) * 2 + b) * block + z * piece, piece)
        full[at, :] = (total / scale).astype(BF16)
        for e in range(1, DEPTH):
            spreads[u, e] = copy(
                full.at[at], full.at[at], gz_sem, (u, e - 1),
                ((z + e) % DEPTH * PLANE + me % PLANE, v),
            )

    def spread(u):
        a, b, by_a, by_b = axes(u)
        for e in range(1, DEPTH):
            spreads[u, e].wait_recv()
        at = rows_at(((u * 2 + a) * 2 + b) * block, block)
        ways = [by_b, by_a] + [by_xy] * (u in DIRECT_SPREAD)
        for i, to in enumerate(ways):
            spreads[u, DEPTH + i] = copy(full.at[at], full.at[at], spread_sem, (u, i), (to, v))

    def forward(u):
        if u in DIRECT_SPREAD:
            return
        a, b, by_a, by_b = axes(u)
        spreads[u, DEPTH].wait_recv()
        at = rows_at(((u * 2 + a) * 2 + 1 - b) * block, block)
        spreads[u, DEPTH + 2] = copy(full.at[at], full.at[at], spread_sem, (u, 2), (by_a, v))

    def done(u):
        if u in DIRECT_SPREAD:
            spreads[u, DEPTH].wait_recv()
        spreads[u, DEPTH + 1].wait_recv()
        spreads[u, DEPTH + 2].wait_recv()
        at = slice(u * unit, (u + 1) * unit)
        return (full[at, :].astype(F32) + gram[at, :]).astype(BF16)

    def energy():
        for t in range(count // 128):
            at = slice(t * 128, (t + 1) * 128)
            line = jnp.broadcast_to(occ_e[t : t + 1, :], (128, 128)).T
            for b in range(width // 128):
                cols = slice(b * 128, (b + 1) * 128)
                acc[at, cols] = (vir_e[:, cols] - line) * amp[at, cols].astype(F32)

    loads[2].wait()
    loads[3].wait()
    cross(0)
    cross(1)

    @pl.when(v == 0)
    def _():
        pl.semaphore_wait(barrier, 1 + 2 * near)
        pl.semaphore_signal(near_sem, inc=1, device_id=(me, 1), device_id_type=MESH)

    @pl.when(v == 1)
    def _():
        pl.semaphore_wait(near_sem, 1)

    sum_first(0)
    sum_first(1)
    amp_copies = []
    for i in range(2):
        at = pl.ds(i * unit, unit)
        amp_copies.append(copy(amp.at[:, at], other.at[:, at], amp_sem, (i,), (me, 1 - v)))
    loads[4].wait()
    loads[5].wait()
    energy()
    sum_second(0)
    sum_second(1)
    amp_copies[0].wait_recv()
    cross(2)
    sum_first(2)

    @pl.when(v == 1)
    def _():
        pl.semaphore_wait(barrier, 1 + 2 * (groups - 1 - near))
        pl.semaphore_signal(far_sem, inc=1, device_id=(me, 0), device_id_type=MESH)

    @pl.when(v == 0)
    def _():
        pl.semaphore_wait(far_sem, 1)

    amp_copies[1].wait_recv()
    cross(3)
    sum_first(3)
    sum_third(0)
    sum_third(1)
    route_copies = []
    for k in range(1, groups):
        to = (me + k) % groups
        route_copies.append(
            copy(outgoing.at[rows_at(to * capacity, capacity)], arr.at[mine], route_sem, (k - 1,), (to, v))
        )
    sum_second(2)
    sum_second(3)
    finish(0)
    finish(1)
    sum_third(2)
    sum_third(3)
    spread(0)
    spread(1)
    for c in route_copies:
        c.wait_recv()
    arr_copy = copy(arr, arr_o, arr_sem, (0,), (me, 1 - v))
    finish(2)
    finish(3)
    forward(0)
    forward(1)
    ladder = math.sqrt(full_width) * math.sqrt(SLOTS)
    contract = (((0,), (0,)), ((), ()))
    gram[:width, :] = lax.dot_general(arr[...], arr[...], contract, preferred_element_type=F32) / ladder
    arr_copy.wait_recv()
    gram[width:, :] = lax.dot_general(arr_o[...], arr[...], contract, preferred_element_type=F32) / ladder
    spread(2)
    spread(3)
    acc[...] += jnp.dot(amp[:, :unit], done(0), preferred_element_type=F32)
    acc[...] += jnp.dot(amp[:, unit:], done(1), preferred_element_type=F32)
    forward(2)
    forward(3)
    acc[...] += jnp.dot(other[:, :unit], done(2), preferred_element_type=F32)
    last[...] = done(3)
    for c in started:
        c.wait_send()


def finish_kernel(other, acc, last, out, held, sem):
    count, width = acc.shape
    unit = last.shape[0]
    tile = 512
    copies = []
    for t in range(count // tile):
        at = slice(t * tile, (t + 1) * tile)
        held[at, :] = (
            acc[at, :] + jnp.dot(other[at, width - unit :], last[...], preferred_element_type=F32)
        ).astype(BF16)
        c = pltpu.make_async_copy(held.at[pl.ds(t * tile, tile)], out.at[pl.ds(t * tile, tile)], sem.at[t])
        c.start()
        copies.append(c)
    for c in copies:
        c.wait()


def fused(amplitudes, cycle_ints, int_rows, row_dest, vir_energy, occ_energy):
    count, width = amplitudes.shape
    groups = DEPTH * PLANE
    unit = 2 * width // UNITS
    block = unit // PLANE
    dma = pltpu.SemaphoreType.DMA
    vmem = pl.BlockSpec(memory_space=pltpu.VMEM)
    other, acc, last = pl.pallas_call(
        kernel,
        out_shape=(
            pltpu.VMEM((count, width), BF16),
            pltpu.VMEM((count, width), F32),
            pltpu.VMEM((unit, width), BF16),
        ),
        in_specs=[pl.BlockSpec(memory_space=pltpu.HBM)] * 6,
        out_specs=[vmem] * 3,
        scratch_shapes=[
            pltpu.VMEM((count, width), BF16),
            pltpu.VMEM((count, width), BF16),
            pltpu.VMEM(int_rows.shape, BF16),
            pltpu.VMEM(row_dest.shape[::-1], jnp.int32),
            pltpu.VMEM((1, width), F32),
            pltpu.VMEM((count // 128, 128), F32),
            pltpu.VMEM((UNITS, unit, width), BF16),
            pltpu.VMEM((UNITS, 2, block, width), BF16),
            pltpu.VMEM((UNITS, block, width), BF16),
            pltpu.VMEM((UNITS, block, width), BF16),
            pltpu.VMEM((UNITS, block, width), BF16),
            pltpu.VMEM((UNITS, DEPTH - 1, block // DEPTH, width), BF16),
            pltpu.VMEM((2 * width, width), BF16),
            pltpu.VMEM((SLOTS, width), BF16),
            pltpu.VMEM((SLOTS, width), BF16),
            pltpu.VMEM((SLOTS, width), BF16),
            pltpu.VMEM((2 * width, width), F32),
            pltpu.SemaphoreType.REGULAR,
            pltpu.SemaphoreType.REGULAR,
            dma((6,)),
            dma((2, 2)),
            dma((2, groups - 1)),
            dma((2, 1)),
            dma((2, UNITS, 3)),
            dma((2, UNITS, DEPTH - 1)),
            dma((2, UNITS, DEPTH - 1)),
            dma((2, UNITS, 3)),
        ],
        compiler_params=pltpu.CompilerParams(
            collective_id=0, has_side_effects=True, vmem_limit_bytes=56 * 2**20
        ),
    )(
        amplitudes, cycle_ints, int_rows, row_dest.T,
        vir_energy.reshape(1, width), occ_energy.reshape(count // 128, 128),
    )
    return pl.pallas_call(
        finish_kernel,
        out_shape=jax.ShapeDtypeStruct((count, width), BF16),
        in_specs=[vmem] * 3,
        out_specs=pl.BlockSpec(memory_space=pltpu.HBM),
        scratch_shapes=[pltpu.VMEM((count, width), BF16), dma((count // 512,))],
        compiler_params=pltpu.CompilerParams(vmem_limit_bytes=24 * 2**20),
    )(other, acc, last)


def solution(mesh):
    fits = mesh.shape["pair"] == DEPTH * PLANE and mesh.shape["vir"] == 2
    return jax.shard_map(
        fused if fits else body,
        mesh=mesh,
        in_specs=(
            P("pair", "vir"),
            P("pair", "vir"),
            P("pair", "vir"),
            P("pair", None),
            P("vir"),
            P("pair"),
        ),
        out_specs=P("pair", "vir"),
        check_vma=False,
    )
```

```python
import math

import jax
import jax.numpy as jnp
from jax import lax
from jax.experimental import pallas as pl
from jax.experimental.pallas import tpu as pltpu
from jax.sharding import PartitionSpec as P

SLOTS = 256


def dispatch(int_rows, row_dest, groups, capacity):
    rows = int_rows.shape[0]
    group = jnp.arange(groups, dtype=jnp.int32)
    member = jnp.any(row_dest[None, :, :] == group[:, None, None], axis=2)
    before = jnp.arange(rows)[:, None] < jnp.arange(rows)[None, :]
    rank = jnp.dot(
        member.astype(jnp.bfloat16), before.astype(jnp.bfloat16), preferred_element_type=jnp.float32
    ).astype(jnp.int32)
    slot = jnp.arange(capacity, dtype=jnp.int32)
    select = member[:, None, :] & (rank[:, None, :] == slot[None, :, None])
    select = select.reshape(groups * capacity, rows).astype(int_rows.dtype)
    return jnp.dot(select, int_rows, preferred_element_type=jnp.float32).astype(int_rows.dtype)


def body(amplitudes, cycle_ints, int_rows, row_dest, vir_energy, occ_energy):
    groups = lax.axis_size("pair")
    row_count, local_width = amplitudes.shape
    full_width = local_width * lax.axis_size("vir")
    capacity = SLOTS // groups
    gathered = lax.all_gather(amplitudes, "vir", axis=1, tiled=True)
    cross_part = lax.dot_general(
        gathered, cycle_ints, (((0,), (0,)), ((), ())), preferred_element_type=jnp.float32
    )
    scale_cycle = math.sqrt(row_count * groups * full_width)
    cross_half = lax.psum((cross_part / scale_cycle).astype(jnp.bfloat16), "pair")
    outgoing = dispatch(int_rows, row_dest, groups, capacity)
    arrived = lax.all_to_all(
        outgoing.reshape(groups, capacity, local_width),
        "pair",
        split_axis=0,
        concat_axis=0,
        tiled=True,
    ).reshape(groups * capacity, local_width)
    chosen = lax.all_gather(arrived, "vir", axis=1, tiled=True)
    coefficient = lax.dot_general(
        gathered, chosen, (((1,), (1,)), ((), ())), preferred_element_type=jnp.float32
    ) / math.sqrt(full_width)
    ladder = jnp.dot(
        coefficient.astype(jnp.bfloat16), arrived, preferred_element_type=jnp.float32
    ) / math.sqrt(SLOTS)
    energy = (vir_energy[None, :] - occ_energy[:, None]) * amplitudes.astype(jnp.float32)
    cycle_term = jnp.dot(gathered, cross_half, preferred_element_type=jnp.float32)
    return (cycle_term + ladder + energy).astype(jnp.bfloat16)


DEPTH, PLANE, UNITS = 4, 4, 4
F32, BF16 = jnp.float32, jnp.bfloat16
MESH = pl.DeviceIdType.MESH


def rows_at(start, size):
    return pl.ds(pl.multiple_of(start, size), size)


def kernel(
    amp_hbm, cyc_hbm, rows_hbm, dest_hbm, vir_hbm, occ_hbm, other, acc, last,
    amp, cyc, rows, dest, vir_e, occ_e, part, first_in, second_in, zsum, z_in, full,
    outgoing, mid, arr, arr_o, gram,
    core_sem, near_sem, hop_sem, load_sem, amp_sem, route_sem, arr_sem, sum_sem, z_sem, gz_sem, spread_sem,
):
    groups = DEPTH * PLANE
    me, v = lax.axis_index("pair"), lax.axis_index("vir")
    z, y, x = me // PLANE, me % PLANE // 2, me % 2
    by_x, by_y, by_xy = me + 1 - 2 * x, me + 2 - 4 * y, z * PLANE + 3 - me % PLANE
    count, width = amp.shape
    full_width = 2 * width
    capacity = SLOTS // groups
    unit = full_width // UNITS
    block = unit // PLANE
    piece = block // DEPTH

    left, right = pl.ds(0, unit), pl.ds(unit, unit)
    loads = [
        pltpu.make_async_copy(src, dst, load_sem.at[i])
        for i, (src, dst) in enumerate(
            (
                (cyc_hbm, cyc), (amp_hbm.at[:, left], amp.at[:, left]), (amp_hbm.at[:, right], amp.at[:, right]),
                (dest_hbm, dest), (rows_hbm, rows), (vir_hbm, vir_e), (occ_hbm, occ_e),
            )
        )
    ]
    for c in loads:
        c.start()

    def signal(sem, to, core):
        pl.semaphore_signal(sem, inc=1, device_id=(to, core), device_id_type=MESH)

    def signal_depth(sem, core):
        @pl.when(z > 0)
        def _():
            signal(sem, me - PLANE, core)

        @pl.when(z < DEPTH - 1)
        def _():
            signal(sem, me + PLANE, core)

    barrier = pltpu.get_barrier_semaphore()

    @pl.when(v == 1)
    def _():
        signal(barrier, me, 0)

    signal(barrier, by_x, 1)
    signal(barrier, by_y, 1)
    signal_depth(barrier, 1)
    ends = jnp.where(z > 0, 1, 0) + jnp.where(z < DEPTH - 1, 1, 0)

    @pl.when(v == 0)
    def _():
        pl.semaphore_wait(barrier, 1)
        signal(core_sem, me, 1)

    @pl.when(v == 1)
    def _():
        pl.semaphore_wait(core_sem, 1)

    started = []

    def copy(src, dst, sem, index, device):
        c = pltpu.make_async_remote_copy(
            src_ref=src,
            dst_ref=dst,
            send_sem=sem.at[(0, *index)],
            recv_sem=sem.at[(1, *index)],
            device_id=device,
            device_id_type=MESH,
        )
        c.start()
        started.append(c)
        return c

    def dispatch():
        group = lax.broadcasted_iota(jnp.int32, (SLOTS, rows.shape[0]), 0) // capacity
        slot = lax.broadcasted_iota(jnp.int32, (SLOTS, rows.shape[0]), 0) % capacity
        member = group == dest[0:1, :]
        for k in range(1, dest.shape[0]):
            member = member | (group == dest[k : k + 1, :])
        tri = (rows.shape[0], rows.shape[0])
        before = lax.broadcasted_iota(jnp.int32, tri, 0) < lax.broadcasted_iota(jnp.int32, tri, 1)
        rank = jnp.dot(
            jnp.where(member, 1.0, 0.0).astype(BF16),
            jnp.where(before, 1.0, 0.0).astype(BF16),
            preferred_element_type=F32,
        )
        select = jnp.where(member & (rank == slot.astype(F32)), 1.0, 0.0).astype(BF16)
        outgoing[...] = jnp.dot(select, rows[...], preferred_element_type=F32).astype(BF16).reshape(outgoing.shape)

    def route_depth():
        mid[z] = outgoing[z]
        return [
            copy(outgoing.at[(z + e) % DEPTH], mid.at[z], route_sem, (0, e - 1), ((z + e) % DEPTH * PLANE + me % PLANE, v))
            for e in range(1, DEPTH)
        ]

    def route_plane():
        for c in routed:
            c.wait_recv()
        q = me % PLANE
        arr[:, q] = mid[:, q]
        return [
            copy(mid.at[:, to % PLANE], arr.at[:, q], route_sem, (1, i), (to, v))
            for i, to in enumerate((by_x, by_y, by_xy))
        ]

    def cross(u):
        src = amp if u < UNITS // 2 else other
        at = u % (UNITS // 2) * unit
        part[u] = lax.dot_general(
            src[:, at : at + unit], cyc[...], (((0,), (0,)), ((), ())), preferred_element_type=F32
        ).astype(BF16)

    def axes(u):
        return (x, y, by_x, by_y) if u % 2 == 0 else (y, x, by_y, by_x)

    def quarter(a, b):
        return rows_at((a * 2 + b) * block, block)

    sums = {}

    def sum_first(u):
        a, b, by_a, by_b = axes(u)
        sums[u, 2] = copy(
            part.at[u, quarter(a, 1 - b)], second_in.at[u], sum_sem, (u, 2), (by_b, v)
        )
        sums[u, 1] = copy(
            part.at[u, quarter(1 - a, b)], first_in.at[u, 1], sum_sem, (u, 1), (by_a, v)
        )

    def sum_across(u):
        a, b, by_a, by_b = axes(u)
        sums[u, 0] = copy(
            part.at[u, quarter(1 - a, 1 - b)], first_in.at[u, 0], sum_sem, (u, 0), (by_xy, v)
        )

    def sum_third(u):
        a, b, by_a, by_b = axes(u)
        total = part[u, quarter(a, b), :].astype(F32)
        sums[u, 1].wait_recv()
        total += first_in[u, 1].astype(F32)
        sums[u, 0].wait_recv()
        total += first_in[u, 0].astype(F32)
        sums[u, 2].wait_recv()
        zsum[u] = (total + second_in[u].astype(F32)).astype(BF16)
        for e in range(1, DEPTH):
            to = (z + e) % DEPTH
            sums[u, 2 + e] = copy(
                zsum.at[u, rows_at(to * piece, piece)], z_in.at[u, e - 1],
                z_sem, (u, e - 1), (to * PLANE + me % PLANE, v),
            )

    scale = math.sqrt(count * groups * full_width)
    spreads = {}

    def finish(u):
        a, b, by_a, by_b = axes(u)
        total = zsum[u, rows_at(z * piece, piece), :].astype(F32)
        for e in range(1, DEPTH):
            sums[u, 2 + e].wait_recv()
            total += z_in[u, e - 1].astype(F32)
        at = rows_at(((u * 2 + a) * 2 + b) * block + z * piece, piece)
        full[at, :] = (total / scale).astype(BF16)
        for e in range(1, DEPTH):
            spreads[u, e] = copy(
                full.at[at], full.at[at], gz_sem, (u, e - 1),
                ((z + e) % DEPTH * PLANE + me % PLANE, v),
            )

    def spread(u):
        a, b, by_a, by_b = axes(u)
        for e in range(1, DEPTH):
            spreads[u, e].wait_recv()
        at = rows_at(((u * 2 + a) * 2 + b) * block, block)
        ways = [by_b, by_a, by_xy]
        for i, to in enumerate(ways):
            spreads[u, DEPTH + i] = copy(full.at[at], full.at[at], spread_sem, (u, i), (to, v))

    def done(u):
        for i in range(3):
            spreads[u, DEPTH + i].wait_recv()
        at = slice(u * unit, (u + 1) * unit)
        return (full[at, :].astype(F32) + gram[at, :]).astype(BF16)

    def energy():
        for t in range(count // 128):
            at = slice(t * 128, (t + 1) * 128)
            line = jnp.broadcast_to(occ_e[t : t + 1, :], (128, 128)).T
            for b in range(width // 128):
                cols = slice(b * 128, (b + 1) * 128)
                acc[at, cols] = (vir_e[:, cols] - line) * amp[at, cols].astype(F32)

    amp_copies = []
    for i, at in enumerate((left, right)):
        amp_copies.append(copy(amp_hbm.at[:, at], other.at[:, at], amp_sem, (i,), (me, 1 - v)))
    loads[0].wait()
    loads[1].wait()
    cross(0)

    @pl.when(v == 1)
    def _():
        pl.semaphore_wait(barrier, 2 * (2 + ends))
        signal(near_sem, me, 0)

    @pl.when(v == 0)
    def _():
        pl.semaphore_wait(near_sem, 1)

    signal(hop_sem.at[0], by_x, v)
    signal(hop_sem.at[0], by_y, v)
    signal_depth(hop_sem.at[0], v)
    sum_first(0)
    loads[2].wait()
    cross(1)
    sum_first(1)
    amp_copies[0].wait_recv()
    cross(2)
    sum_first(2)
    pl.semaphore_wait(hop_sem.at[0], 2 + ends)
    signal_depth(hop_sem.at[1], v)
    sum_across(0)
    sum_across(1)
    sum_across(2)
    for c in loads[3:]:
        c.wait()
    dispatch()
    amp_copies[1].wait_recv()
    cross(3)
    sum_first(3)
    sum_across(3)
    pl.semaphore_wait(hop_sem.at[1], ends)
    routed = route_depth()
    energy()
    sum_third(0)
    sum_third(1)
    finish(0)
    finish(1)
    sum_third(2)
    sum_third(3)
    routed = route_plane()
    spread(0)
    spread(1)
    finish(2)
    finish(3)
    for c in routed:
        c.wait_recv()
    arr_copy = copy(arr, arr_o, arr_sem, (0,), (me, 1 - v))
    ladder = math.sqrt(full_width) * math.sqrt(SLOTS)
    contract = (((0,), (0,)), ((), ()))
    chosen = arr[...].reshape(SLOTS, width)
    gram[:width, :] = lax.dot_general(chosen, chosen, contract, preferred_element_type=F32) / ladder
    spread(2)
    spread(3)
    arr_copy.wait_recv()
    chosen_o = arr_o[...].reshape(SLOTS, width)
    gram[width:, :] = lax.dot_general(chosen_o, chosen, contract, preferred_element_type=F32) / ladder
    acc[...] += jnp.dot(amp[:, :unit], done(0), preferred_element_type=F32)
    acc[...] += jnp.dot(amp[:, unit:], done(1), preferred_element_type=F32)
    acc[...] += jnp.dot(other[:, :unit], done(2), preferred_element_type=F32)
    last[...] = done(3)
    for c in started:
        c.wait_send()


def finish_kernel(other, acc, last, out, held, sem):
    count, width = acc.shape
    unit = last.shape[0]
    tile = 512
    copies = []
    for t in range(count // tile):
        at = slice(t * tile, (t + 1) * tile)
        held[at, :] = (
            acc[at, :] + jnp.dot(other[at, width - unit :], last[...], preferred_element_type=F32)
        ).astype(BF16)
        c = pltpu.make_async_copy(held.at[pl.ds(t * tile, tile)], out.at[pl.ds(t * tile, tile)], sem.at[t])
        c.start()
        copies.append(c)
    for c in copies:
        c.wait()


def fused(amplitudes, cycle_ints, int_rows, row_dest, vir_energy, occ_energy):
    count, width = amplitudes.shape
    groups = DEPTH * PLANE
    unit = 2 * width // UNITS
    block = unit // PLANE
    dma = pltpu.SemaphoreType.DMA
    vmem = pl.BlockSpec(memory_space=pltpu.VMEM)
    other, acc, last = pl.pallas_call(
        kernel,
        out_shape=(
            pltpu.VMEM((count, width), BF16),
            pltpu.VMEM((count, width), F32),
            pltpu.VMEM((unit, width), BF16),
        ),
        in_specs=[pl.BlockSpec(memory_space=pltpu.HBM)] * 6,
        out_specs=[vmem] * 3,
        scratch_shapes=[
            pltpu.VMEM((count, width), BF16),
            pltpu.VMEM((count, width), BF16),
            pltpu.VMEM(int_rows.shape, BF16),
            pltpu.VMEM(row_dest.shape[::-1], jnp.int32),
            pltpu.VMEM((1, width), F32),
            pltpu.VMEM((count // 128, 128), F32),
            pltpu.VMEM((UNITS, unit, width), BF16),
            pltpu.VMEM((UNITS, 2, block, width), BF16),
            pltpu.VMEM((UNITS, block, width), BF16),
            pltpu.VMEM((UNITS, block, width), BF16),
            pltpu.VMEM((UNITS, DEPTH - 1, block // DEPTH, width), BF16),
            pltpu.VMEM((2 * width, width), BF16),
            pltpu.VMEM((DEPTH, PLANE, SLOTS // groups, width), BF16),
            pltpu.VMEM((DEPTH, PLANE, SLOTS // groups, width), BF16),
            pltpu.VMEM((DEPTH, PLANE, SLOTS // groups, width), BF16),
            pltpu.VMEM((DEPTH, PLANE, SLOTS // groups, width), BF16),
            pltpu.VMEM((2 * width, width), F32),
            pltpu.SemaphoreType.REGULAR,
            pltpu.SemaphoreType.REGULAR,
            pltpu.SemaphoreType.REGULAR((2,)),
            dma((7,)),
            dma((2, 2)),
            dma((2, 2, 3)),
            dma((2, 1)),
            dma((2, UNITS, 3)),
            dma((2, UNITS, DEPTH - 1)),
            dma((2, UNITS, DEPTH - 1)),
            dma((2, UNITS, 3)),
        ],
        compiler_params=pltpu.CompilerParams(
            collective_id=0, has_side_effects=True, vmem_limit_bytes=56 * 2**20
        ),
    )(
        amplitudes, cycle_ints, int_rows, row_dest.T,
        vir_energy.reshape(1, width), occ_energy.reshape(count // 128, 128),
    )
    return pl.pallas_call(
        finish_kernel,
        out_shape=jax.ShapeDtypeStruct((count, width), BF16),
        in_specs=[vmem] * 3,
        out_specs=pl.BlockSpec(memory_space=pltpu.HBM),
        scratch_shapes=[pltpu.VMEM((count, width), BF16), dma((count // 512,))],
        compiler_params=pltpu.CompilerParams(vmem_limit_bytes=24 * 2**20),
    )(other, acc, last)


def solution(mesh):
    fits = mesh.shape["pair"] == DEPTH * PLANE and mesh.shape["vir"] == 2
    return jax.shard_map(
        fused if fits else body,
        mesh=mesh,
        in_specs=(
            P("pair", "vir"),
            P("pair", "vir"),
            P("pair", "vir"),
            P("pair", None),
            P("vir"),
            P("pair"),
        ),
        out_specs=P("pair", "vir"),
        check_vma=False,
    )
```

```python
import math

import jax
import jax.numpy as jnp
from jax import lax
from jax.experimental import pallas as pl
from jax.experimental.pallas import tpu as pltpu
from jax.sharding import PartitionSpec as P

SLOTS = 256


def dispatch(int_rows, row_dest, groups, capacity):
    rows = int_rows.shape[0]
    group = jnp.arange(groups, dtype=jnp.int32)
    member = jnp.any(row_dest[None, :, :] == group[:, None, None], axis=2)
    before = jnp.arange(rows)[:, None] < jnp.arange(rows)[None, :]
    rank = jnp.dot(
        member.astype(jnp.bfloat16), before.astype(jnp.bfloat16), preferred_element_type=jnp.float32
    ).astype(jnp.int32)
    slot = jnp.arange(capacity, dtype=jnp.int32)
    select = member[:, None, :] & (rank[:, None, :] == slot[None, :, None])
    select = select.reshape(groups * capacity, rows).astype(int_rows.dtype)
    return jnp.dot(select, int_rows, preferred_element_type=jnp.float32).astype(int_rows.dtype)


def body(amplitudes, cycle_ints, int_rows, row_dest, vir_energy, occ_energy):
    groups = lax.axis_size("pair")
    row_count, local_width = amplitudes.shape
    full_width = local_width * lax.axis_size("vir")
    capacity = SLOTS // groups
    gathered = lax.all_gather(amplitudes, "vir", axis=1, tiled=True)
    cross_part = lax.dot_general(
        gathered, cycle_ints, (((0,), (0,)), ((), ())), preferred_element_type=jnp.float32
    )
    scale_cycle = math.sqrt(row_count * groups * full_width)
    cross_half = lax.psum((cross_part / scale_cycle).astype(jnp.bfloat16), "pair")
    outgoing = dispatch(int_rows, row_dest, groups, capacity)
    arrived = lax.all_to_all(
        outgoing.reshape(groups, capacity, local_width),
        "pair",
        split_axis=0,
        concat_axis=0,
        tiled=True,
    ).reshape(groups * capacity, local_width)
    chosen = lax.all_gather(arrived, "vir", axis=1, tiled=True)
    coefficient = lax.dot_general(
        gathered, chosen, (((1,), (1,)), ((), ())), preferred_element_type=jnp.float32
    ) / math.sqrt(full_width)
    ladder = jnp.dot(
        coefficient.astype(jnp.bfloat16), arrived, preferred_element_type=jnp.float32
    ) / math.sqrt(SLOTS)
    energy = (vir_energy[None, :] - occ_energy[:, None]) * amplitudes.astype(jnp.float32)
    cycle_term = jnp.dot(gathered, cross_half, preferred_element_type=jnp.float32)
    return (cycle_term + ladder + energy).astype(jnp.bfloat16)


DEPTH, PLANE, UNITS = 4, 4, 4
F32, BF16 = jnp.float32, jnp.bfloat16
MESH = pl.DeviceIdType.MESH


def rows_at(start, size):
    return pl.ds(pl.multiple_of(start, size), size)


def kernel(
    amp_hbm, cyc_hbm, rows_hbm, dest_hbm, vir_hbm, occ_hbm, other, acc, last,
    amp, cyc, rows, dest, vir_e, occ_e, part, first_in, second_in, zsum, z_in, full,
    outgoing, mid, arr, arr_o, gram,
    core_sem, near_sem, hop_sem, load_sem, amp_sem, route_sem, arr_sem, sum_sem, z_sem, gz_sem, spread_sem,
):
    groups = DEPTH * PLANE
    me, v = lax.axis_index("pair"), lax.axis_index("vir")
    z, y, x = me // PLANE, me % PLANE // 2, me % 2
    by_x, by_y, by_xy = me + 1 - 2 * x, me + 2 - 4 * y, z * PLANE + 3 - me % PLANE
    count, width = amp.shape
    full_width = 2 * width
    capacity = SLOTS // groups
    unit = full_width // UNITS
    block = unit // PLANE
    piece = block // DEPTH

    left, right = pl.ds(0, unit), pl.ds(unit, unit)
    loads = [
        pltpu.make_async_copy(src, dst, load_sem.at[i])
        for i, (src, dst) in enumerate(
            (
                (cyc_hbm, cyc), (amp_hbm.at[:, left], amp.at[:, left]), (amp_hbm.at[:, right], amp.at[:, right]),
                (dest_hbm, dest), (rows_hbm, rows), (vir_hbm, vir_e), (occ_hbm, occ_e),
            )
        )
    ]
    for c in loads:
        c.start()

    def signal(sem, to, core):
        pl.semaphore_signal(sem, inc=1, device_id=(to, core), device_id_type=MESH)

    def signal_depth(sem, core):
        @pl.when(z > 0)
        def _():
            signal(sem, me - PLANE, core)

        @pl.when(z < DEPTH - 1)
        def _():
            signal(sem, me + PLANE, core)

    barrier = pltpu.get_barrier_semaphore()

    @pl.when(v == 1)
    def _():
        signal(barrier, me, 0)

    signal(barrier, by_x, 1)
    signal(barrier, by_y, 1)
    signal_depth(barrier, 1)
    ends = jnp.where(z > 0, 1, 0) + jnp.where(z < DEPTH - 1, 1, 0)

    @pl.when(v == 0)
    def _():
        pl.semaphore_wait(barrier, 1)
        signal(core_sem, me, 1)

    @pl.when(v == 1)
    def _():
        pl.semaphore_wait(core_sem, 1)

    started = []

    def copy(src, dst, sem, index, device):
        c = pltpu.make_async_remote_copy(
            src_ref=src,
            dst_ref=dst,
            send_sem=sem.at[(0, *index)],
            recv_sem=sem.at[(1, *index)],
            device_id=device,
            device_id_type=MESH,
        )
        c.start()
        started.append(c)
        return c

    def dispatch():
        group = lax.broadcasted_iota(jnp.int32, (SLOTS, rows.shape[0]), 0) // capacity
        slot = lax.broadcasted_iota(jnp.int32, (SLOTS, rows.shape[0]), 0) % capacity
        member = group == dest[0:1, :]
        for k in range(1, dest.shape[0]):
            member = member | (group == dest[k : k + 1, :])
        tri = (rows.shape[0], rows.shape[0])
        before = lax.broadcasted_iota(jnp.int32, tri, 0) < lax.broadcasted_iota(jnp.int32, tri, 1)
        rank = jnp.dot(
            jnp.where(member, 1.0, 0.0).astype(BF16),
            jnp.where(before, 1.0, 0.0).astype(BF16),
            preferred_element_type=F32,
        )
        select = jnp.where(member & (rank == slot.astype(F32)), 1.0, 0.0).astype(BF16)
        outgoing[...] = jnp.dot(select, rows[...], preferred_element_type=F32).astype(BF16).reshape(outgoing.shape)

    routed = []

    def route_depth(i):
        to = (z + 1 - 2 * (z % 2), (z + 2) % DEPTH, DEPTH - 1 - z)[i]
        routed.append(
            copy(outgoing.at[to], mid.at[z], route_sem, (0, i), (to * PLANE + me % PLANE, v))
        )

    def route_plane():
        for c in routed:
            c.wait_recv()
        q = me % PLANE
        mid[z] = outgoing[z]
        arr[:, q] = mid[:, q]
        return [
            copy(mid.at[:, to % PLANE], arr.at[:, q], route_sem, (1, i), (to, v))
            for i, to in enumerate((by_x, by_y, by_xy))
        ]

    def cross(u):
        src = amp if u < UNITS // 2 else other
        at = u % (UNITS // 2) * unit
        part[u] = lax.dot_general(
            src[:, at : at + unit], cyc[...], (((0,), (0,)), ((), ())), preferred_element_type=F32
        ).astype(BF16)

    def axes(u):
        return (x, y, by_x, by_y) if u % 2 == 0 else (y, x, by_y, by_x)

    def quarter(a, b):
        return rows_at((a * 2 + b) * block, block)

    sums = {}

    def sum_first(u):
        a, b, by_a, by_b = axes(u)
        sums[u, 2] = copy(
            part.at[u, quarter(a, 1 - b)], second_in.at[u], sum_sem, (u, 2), (by_b, v)
        )
        sums[u, 1] = copy(
            part.at[u, quarter(1 - a, b)], first_in.at[u, 1], sum_sem, (u, 1), (by_a, v)
        )

    def sum_across(u):
        a, b, by_a, by_b = axes(u)
        sums[u, 0] = copy(
            part.at[u, quarter(1 - a, 1 - b)], first_in.at[u, 0], sum_sem, (u, 0), (by_xy, v)
        )

    def sum_third(u):
        a, b, by_a, by_b = axes(u)
        total = part[u, quarter(a, b), :].astype(F32)
        sums[u, 1].wait_recv()
        total += first_in[u, 1].astype(F32)
        sums[u, 0].wait_recv()
        total += first_in[u, 0].astype(F32)
        sums[u, 2].wait_recv()
        zsum[u] = (total + second_in[u].astype(F32)).astype(BF16)
        for e in range(1, DEPTH):
            to = (z + e) % DEPTH
            sums[u, 2 + e] = copy(
                zsum.at[u, rows_at(to * piece, piece)], z_in.at[u, e - 1],
                z_sem, (u, e - 1), (to * PLANE + me % PLANE, v),
            )

    scale = math.sqrt(count * groups * full_width)
    spreads = {}

    def finish(u):
        a, b, by_a, by_b = axes(u)
        total = zsum[u, rows_at(z * piece, piece), :].astype(F32)
        for e in range(1, DEPTH):
            sums[u, 2 + e].wait_recv()
            total += z_in[u, e - 1].astype(F32)
        at = rows_at(((u * 2 + a) * 2 + b) * block + z * piece, piece)
        full[at, :] = (total / scale).astype(BF16)
        for e in range(1, DEPTH):
            spreads[u, e] = copy(
                full.at[at], full.at[at], gz_sem, (u, e - 1),
                ((z + e) % DEPTH * PLANE + me % PLANE, v),
            )

    def spread(u):
        a, b, by_a, by_b = axes(u)
        for e in range(1, DEPTH):
            spreads[u, e].wait_recv()
        at = rows_at(((u * 2 + a) * 2 + b) * block, block)
        ways = [by_b, by_a, by_xy]
        for i, to in enumerate(ways):
            spreads[u, DEPTH + i] = copy(full.at[at], full.at[at], spread_sem, (u, i), (to, v))

    def done(u):
        for i in range(3):
            spreads[u, DEPTH + i].wait_recv()
        at = slice(u * unit, (u + 1) * unit)
        return (full[at, :].astype(F32) + gram[at, :]).astype(BF16)

    def energy():
        for t in range(count // 128):
            at = slice(t * 128, (t + 1) * 128)
            line = jnp.broadcast_to(occ_e[t : t + 1, :], (128, 128)).T
            for b in range(width // 128):
                cols = slice(b * 128, (b + 1) * 128)
                acc[at, cols] = (vir_e[:, cols] - line) * amp[at, cols].astype(F32)

    amp_copies = []
    for i, at in enumerate((left, right)):
        amp_copies.append(copy(amp_hbm.at[:, at], other.at[:, at], amp_sem, (i,), (me, 1 - v)))
    loads[0].wait()
    loads[1].wait()
    cross(0)

    @pl.when(v == 1)
    def _():
        pl.semaphore_wait(barrier, 2 * (2 + ends))
        signal(near_sem, me, 0)

    @pl.when(v == 0)
    def _():
        pl.semaphore_wait(near_sem, 1)

    signal(hop_sem.at[0], by_x, v)
    signal(hop_sem.at[0], by_y, v)
    signal_depth(hop_sem.at[0], v)
    sum_first(0)
    loads[2].wait()
    cross(1)
    sum_first(1)
    for c in loads[3:]:
        c.wait()
    dispatch()
    route_depth(0)
    pl.semaphore_wait(hop_sem.at[0], 2 + ends)
    signal_depth(hop_sem.at[1], v)
    route_depth(1)
    sum_across(0)
    amp_copies[0].wait_recv()
    cross(2)
    sum_first(2)
    sum_across(1)
    sum_across(2)
    pl.semaphore_wait(hop_sem.at[1], ends)
    route_depth(2)
    amp_copies[1].wait_recv()
    cross(3)
    sum_first(3)
    sum_across(3)
    sum_third(0)
    energy()
    routed = route_plane()
    sum_third(1)
    sum_third(2)
    finish(0)
    finish(1)
    sum_third(3)
    spread(0)
    spread(1)
    for c in routed:
        c.wait_recv()
    arr_copy = copy(arr, arr_o, arr_sem, (0,), (me, 1 - v))
    ladder = math.sqrt(full_width) * math.sqrt(SLOTS)
    contract = (((0,), (0,)), ((), ()))
    chosen = arr[...].reshape(SLOTS, width)
    gram[:width, :] = lax.dot_general(chosen, chosen, contract, preferred_element_type=F32) / ladder
    finish(2)
    finish(3)
    spread(2)
    spread(3)
    arr_copy.wait_recv()
    chosen_o = arr_o[...].reshape(SLOTS, width)
    gram[width:, :] = lax.dot_general(chosen_o, chosen, contract, preferred_element_type=F32) / ladder
    acc[...] += jnp.dot(amp[:, :unit], done(0), preferred_element_type=F32)
    acc[...] += jnp.dot(amp[:, unit:], done(1), preferred_element_type=F32)
    acc[...] += jnp.dot(other[:, :unit], done(2), preferred_element_type=F32)
    last[...] = done(3)
    for c in started:
        c.wait_send()


def finish_kernel(other, acc, last, out, held, sem):
    count, width = acc.shape
    unit = last.shape[0]
    tile = 512
    copies = []
    for t in range(count // tile):
        at = slice(t * tile, (t + 1) * tile)
        held[at, :] = (
            acc[at, :] + jnp.dot(other[at, width - unit :], last[...], preferred_element_type=F32)
        ).astype(BF16)
        c = pltpu.make_async_copy(held.at[pl.ds(t * tile, tile)], out.at[pl.ds(t * tile, tile)], sem.at[t])
        c.start()
        copies.append(c)
    for c in copies:
        c.wait()


def fused(amplitudes, cycle_ints, int_rows, row_dest, vir_energy, occ_energy):
    count, width = amplitudes.shape
    groups = DEPTH * PLANE
    unit = 2 * width // UNITS
    block = unit // PLANE
    dma = pltpu.SemaphoreType.DMA
    vmem = pl.BlockSpec(memory_space=pltpu.VMEM)
    other, acc, last = pl.pallas_call(
        kernel,
        out_shape=(
            pltpu.VMEM((count, width), BF16),
            pltpu.VMEM((count, width), F32),
            pltpu.VMEM((unit, width), BF16),
        ),
        in_specs=[pl.BlockSpec(memory_space=pltpu.HBM)] * 6,
        out_specs=[vmem] * 3,
        scratch_shapes=[
            pltpu.VMEM((count, width), BF16),
            pltpu.VMEM((count, width), BF16),
            pltpu.VMEM(int_rows.shape, BF16),
            pltpu.VMEM(row_dest.shape[::-1], jnp.int32),
            pltpu.VMEM((1, width), F32),
            pltpu.VMEM((count // 128, 128), F32),
            pltpu.VMEM((UNITS, unit, width), BF16),
            pltpu.VMEM((UNITS, 2, block, width), BF16),
            pltpu.VMEM((UNITS, block, width), BF16),
            pltpu.VMEM((UNITS, block, width), BF16),
            pltpu.VMEM((UNITS, DEPTH - 1, block // DEPTH, width), BF16),
            pltpu.VMEM((2 * width, width), BF16),
            pltpu.VMEM((DEPTH, PLANE, SLOTS // groups, width), BF16),
            pltpu.VMEM((DEPTH, PLANE, SLOTS // groups, width), BF16),
            pltpu.VMEM((DEPTH, PLANE, SLOTS // groups, width), BF16),
            pltpu.VMEM((DEPTH, PLANE, SLOTS // groups, width), BF16),
            pltpu.VMEM((2 * width, width), F32),
            pltpu.SemaphoreType.REGULAR,
            pltpu.SemaphoreType.REGULAR,
            pltpu.SemaphoreType.REGULAR((2,)),
            dma((7,)),
            dma((2, 2)),
            dma((2, 2, 3)),
            dma((2, 1)),
            dma((2, UNITS, 3)),
            dma((2, UNITS, DEPTH - 1)),
            dma((2, UNITS, DEPTH - 1)),
            dma((2, UNITS, 3)),
        ],
        compiler_params=pltpu.CompilerParams(
            collective_id=0, has_side_effects=True, vmem_limit_bytes=56 * 2**20
        ),
    )(
        amplitudes, cycle_ints, int_rows, row_dest.T,
        vir_energy.reshape(1, width), occ_energy.reshape(count // 128, 128),
    )
    return pl.pallas_call(
        finish_kernel,
        out_shape=jax.ShapeDtypeStruct((count, width), BF16),
        in_specs=[vmem] * 3,
        out_specs=pl.BlockSpec(memory_space=pltpu.HBM),
        scratch_shapes=[pltpu.VMEM((count, width), BF16), dma((count // 512,))],
        compiler_params=pltpu.CompilerParams(vmem_limit_bytes=24 * 2**20),
    )(other, acc, last)


def solution(mesh):
    fits = mesh.shape["pair"] == DEPTH * PLANE and mesh.shape["vir"] == 2
    return jax.shard_map(
        fused if fits else body,
        mesh=mesh,
        in_specs=(
            P("pair", "vir"),
            P("pair", "vir"),
            P("pair", "vir"),
            P("pair", None),
            P("vir"),
            P("pair"),
        ),
        out_specs=P("pair", "vir"),
        check_vma=False,
    )
```

```python
import math

import jax
import jax.numpy as jnp
from jax import lax
from jax.experimental import pallas as pl
from jax.experimental.pallas import tpu as pltpu
from jax.sharding import PartitionSpec as P

SLOTS = 256


def dispatch(int_rows, row_dest, groups, capacity):
    rows = int_rows.shape[0]
    group = jnp.arange(groups, dtype=jnp.int32)
    member = jnp.any(row_dest[None, :, :] == group[:, None, None], axis=2)
    before = jnp.arange(rows)[:, None] < jnp.arange(rows)[None, :]
    rank = jnp.dot(
        member.astype(jnp.bfloat16), before.astype(jnp.bfloat16), preferred_element_type=jnp.float32
    ).astype(jnp.int32)
    slot = jnp.arange(capacity, dtype=jnp.int32)
    select = member[:, None, :] & (rank[:, None, :] == slot[None, :, None])
    select = select.reshape(groups * capacity, rows).astype(int_rows.dtype)
    return jnp.dot(select, int_rows, preferred_element_type=jnp.float32).astype(int_rows.dtype)


def body(amplitudes, cycle_ints, int_rows, row_dest, vir_energy, occ_energy):
    groups = lax.axis_size("pair")
    row_count, local_width = amplitudes.shape
    full_width = local_width * lax.axis_size("vir")
    capacity = SLOTS // groups
    gathered = lax.all_gather(amplitudes, "vir", axis=1, tiled=True)
    cross_part = lax.dot_general(
        gathered, cycle_ints, (((0,), (0,)), ((), ())), preferred_element_type=jnp.float32
    )
    scale_cycle = math.sqrt(row_count * groups * full_width)
    cross_half = lax.psum((cross_part / scale_cycle).astype(jnp.bfloat16), "pair")
    outgoing = dispatch(int_rows, row_dest, groups, capacity)
    arrived = lax.all_to_all(
        outgoing.reshape(groups, capacity, local_width),
        "pair",
        split_axis=0,
        concat_axis=0,
        tiled=True,
    ).reshape(groups * capacity, local_width)
    chosen = lax.all_gather(arrived, "vir", axis=1, tiled=True)
    coefficient = lax.dot_general(
        gathered, chosen, (((1,), (1,)), ((), ())), preferred_element_type=jnp.float32
    ) / math.sqrt(full_width)
    ladder = jnp.dot(
        coefficient.astype(jnp.bfloat16), arrived, preferred_element_type=jnp.float32
    ) / math.sqrt(SLOTS)
    energy = (vir_energy[None, :] - occ_energy[:, None]) * amplitudes.astype(jnp.float32)
    cycle_term = jnp.dot(gathered, cross_half, preferred_element_type=jnp.float32)
    return (cycle_term + ladder + energy).astype(jnp.bfloat16)


DEPTH, PLANE, UNITS = 4, 4, 4
F32, BF16 = jnp.float32, jnp.bfloat16
MESH = pl.DeviceIdType.MESH


def rows_at(start, size):
    return pl.ds(pl.multiple_of(start, size), size)


def kernel(
    amp_hbm, cyc_hbm, rows_hbm, dest_hbm, vir_hbm, occ_hbm, other, acc, last,
    amp, cyc, rows, dest, vir_e, occ_e, part, first_in, second_in, zsum, z_in, full,
    outgoing, mid, arr, arr_o, gram,
    core_sem, near_sem, hop_sem, load_sem, amp_sem, route_sem, arr_sem, sum_sem, z_sem, gz_sem, spread_sem,
):
    groups = DEPTH * PLANE
    me, v = lax.axis_index("pair"), lax.axis_index("vir")
    z, y, x = me // PLANE, me % PLANE // 2, me % 2
    by_x, by_y, by_xy = me + 1 - 2 * x, me + 2 - 4 * y, z * PLANE + 3 - me % PLANE
    count, width = amp.shape
    full_width = 2 * width
    capacity = SLOTS // groups
    unit = full_width // UNITS
    block = unit // PLANE
    piece = block // DEPTH

    left, right = pl.ds(0, unit), pl.ds(unit, unit)
    loads = [
        pltpu.make_async_copy(src, dst, load_sem.at[i])
        for i, (src, dst) in enumerate(
            (
                (cyc_hbm, cyc), (amp_hbm.at[:, left], amp.at[:, left]), (amp_hbm.at[:, right], amp.at[:, right]),
                (dest_hbm, dest), (rows_hbm, rows), (vir_hbm, vir_e), (occ_hbm, occ_e),
            )
        )
    ]
    for c in loads:
        c.start()

    def signal(sem, to, core):
        pl.semaphore_signal(sem, inc=1, device_id=(to, core), device_id_type=MESH)

    def signal_depth(sem, core):
        @pl.when(z > 0)
        def _():
            signal(sem, me - PLANE, core)

        @pl.when(z < DEPTH - 1)
        def _():
            signal(sem, me + PLANE, core)

    barrier = pltpu.get_barrier_semaphore()

    @pl.when(v == 1)
    def _():
        signal(barrier, me, 0)

    signal(barrier, by_x, 1)
    signal(barrier, by_y, 1)
    signal_depth(barrier, 1)
    ends = jnp.where(z > 0, 1, 0) + jnp.where(z < DEPTH - 1, 1, 0)

    @pl.when(v == 0)
    def _():
        pl.semaphore_wait(barrier, 1)
        signal(core_sem, me, 1)

    @pl.when(v == 1)
    def _():
        pl.semaphore_wait(core_sem, 1)

    started = []

    def copy(src, dst, sem, index, device):
        c = pltpu.make_async_remote_copy(
            src_ref=src,
            dst_ref=dst,
            send_sem=sem.at[(0, *index)],
            recv_sem=sem.at[(1, *index)],
            device_id=device,
            device_id_type=MESH,
        )
        c.start()
        started.append(c)
        return c

    def dispatch():
        group = lax.broadcasted_iota(jnp.int32, (SLOTS, rows.shape[0]), 0) // capacity
        slot = lax.broadcasted_iota(jnp.int32, (SLOTS, rows.shape[0]), 0) % capacity
        member = group == dest[0:1, :]
        for k in range(1, dest.shape[0]):
            member = member | (group == dest[k : k + 1, :])
        tri = (rows.shape[0], rows.shape[0])
        before = lax.broadcasted_iota(jnp.int32, tri, 0) < lax.broadcasted_iota(jnp.int32, tri, 1)
        rank = jnp.dot(
            jnp.where(member, 1.0, 0.0).astype(BF16),
            jnp.where(before, 1.0, 0.0).astype(BF16),
            preferred_element_type=F32,
        )
        select = jnp.where(member & (rank == slot.astype(F32)), 1.0, 0.0).astype(BF16)
        outgoing[...] = jnp.dot(select, rows[...], preferred_element_type=F32).astype(BF16).reshape(outgoing.shape)

    routed = []

    def route_depth(i):
        to = (z + 1 - 2 * (z % 2), (z + 2) % DEPTH, DEPTH - 1 - z)[i]
        routed.append(
            copy(outgoing.at[to], mid.at[z], route_sem, (0, i), (to * PLANE + me % PLANE, v))
        )

    def route_plane():
        for c in routed:
            c.wait_recv()
        q = me % PLANE
        mid[z] = outgoing[z]
        arr[:, q] = mid[:, q]
        return [
            copy(mid.at[:, to % PLANE], arr.at[:, q], route_sem, (1, i), (to, v))
            for i, to in enumerate((by_x, by_y, by_xy))
        ]

    def cross(u):
        src = amp if u < UNITS // 2 else other
        at = u % (UNITS // 2) * unit
        part[u] = lax.dot_general(
            src[:, at : at + unit], cyc[...], (((0,), (0,)), ((), ())), preferred_element_type=F32
        ).astype(BF16)

    def axes(u):
        return (x, y, by_x, by_y) if u % 2 == 0 else (y, x, by_y, by_x)

    def quarter(a, b):
        return rows_at((a * 2 + b) * block, block)

    sums = {}

    def sum_first(u):
        a, b, by_a, by_b = axes(u)
        sums[u, 2] = copy(
            part.at[u, quarter(a, 1 - b)], second_in.at[u], sum_sem, (u, 2), (by_b, v)
        )
        sums[u, 1] = copy(
            part.at[u, quarter(1 - a, b)], first_in.at[u, 1], sum_sem, (u, 1), (by_a, v)
        )

    def sum_across(u):
        a, b, by_a, by_b = axes(u)
        sums[u, 0] = copy(
            part.at[u, quarter(1 - a, 1 - b)], first_in.at[u, 0], sum_sem, (u, 0), (by_xy, v)
        )

    def sum_third(u):
        a, b, by_a, by_b = axes(u)
        total = part[u, quarter(a, b), :].astype(F32)
        sums[u, 1].wait_recv()
        total += first_in[u, 1].astype(F32)
        sums[u, 0].wait_recv()
        total += first_in[u, 0].astype(F32)
        sums[u, 2].wait_recv()
        zsum[u] = (total + second_in[u].astype(F32)).astype(BF16)
        for e in range(1, DEPTH):
            to = (z + e) % DEPTH
            sums[u, 2 + e] = copy(
                zsum.at[u, rows_at(to * piece, piece)], z_in.at[u, e - 1],
                z_sem, (u, e - 1), (to * PLANE + me % PLANE, v),
            )

    scale = math.sqrt(count * groups * full_width)
    spreads, planes = {}, {}

    def finish(u):
        a, b, by_a, by_b = axes(u)
        total = zsum[u, rows_at(z * piece, piece), :].astype(F32)
        for e in range(1, DEPTH):
            sums[u, 2 + e].wait_recv()
            total += z_in[u, e - 1].astype(F32)
        at = rows_at(((u * 2 + a) * 2 + b) * block + z * piece, piece)
        full[at, :] = (total / scale).astype(BF16)
        for e in range(1, DEPTH):
            spreads[u, e] = copy(
                full.at[at], full.at[at], gz_sem, (u, e - 1),
                ((z + e) % DEPTH * PLANE + me % PLANE, v),
            )

    def spread(u, e):
        a, b, by_a, by_b = axes(u)
        if e:
            spreads[u, e].wait_recv()
        at = rows_at(((u * 2 + a) * 2 + b) * block + (z - e + DEPTH) % DEPTH * piece, piece)
        for i, to in enumerate((by_b, by_a, by_xy)):
            planes[u, e, i] = copy(full.at[at], full.at[at], spread_sem, (u, e, i), (to, v))

    def done(u):
        for e in range(DEPTH):
            for i in range(PLANE - 1):
                planes[u, e, i].wait_recv()
        at = slice(u * unit, (u + 1) * unit)
        return (full[at, :].astype(F32) + gram[at, :]).astype(BF16)

    def energy():
        for t in range(count // 128):
            at = slice(t * 128, (t + 1) * 128)
            line = jnp.broadcast_to(occ_e[t : t + 1, :], (128, 128)).T
            for b in range(width // 128):
                cols = slice(b * 128, (b + 1) * 128)
                acc[at, cols] = (vir_e[:, cols] - line) * amp[at, cols].astype(F32)

    amp_copies = []
    for i, at in enumerate((left, right)):
        amp_copies.append(copy(amp_hbm.at[:, at], other.at[:, at], amp_sem, (i,), (me, 1 - v)))
    loads[0].wait()
    loads[1].wait()
    cross(0)

    @pl.when(v == 1)
    def _():
        pl.semaphore_wait(barrier, 2 * (2 + ends))
        signal(near_sem, me, 0)

    @pl.when(v == 0)
    def _():
        pl.semaphore_wait(near_sem, 1)

    signal(hop_sem.at[0], by_x, v)
    signal(hop_sem.at[0], by_y, v)
    signal_depth(hop_sem.at[0], v)
    sum_first(0)
    loads[2].wait()
    cross(1)
    sum_first(1)
    pl.semaphore_wait(hop_sem.at[0], 2 + ends)
    signal_depth(hop_sem.at[1], v)
    sum_across(0)
    sum_across(1)
    for c in loads[3:]:
        c.wait()
    dispatch()
    route_depth(0)
    route_depth(1)
    amp_copies[0].wait_recv()
    cross(2)
    sum_first(2)
    sum_across(2)
    pl.semaphore_wait(hop_sem.at[1], ends)
    route_depth(2)
    amp_copies[1].wait_recv()
    cross(3)
    sum_first(3)
    sum_across(3)
    sum_third(0)
    routed = route_plane()
    sum_third(1)
    energy()
    sum_third(2)
    finish(0)
    spread(0, 0)
    finish(1)
    spread(1, 0)
    sum_third(3)
    finish(2)
    spread(2, 0)
    for e in range(1, DEPTH):
        spread(0, e)
    for e in range(1, DEPTH):
        spread(1, e)
    finish(3)
    spread(3, 0)
    for c in routed:
        c.wait_recv()
    arr_copy = copy(arr, arr_o, arr_sem, (0,), (me, 1 - v))
    ladder = math.sqrt(full_width) * math.sqrt(SLOTS)
    contract = (((0,), (0,)), ((), ()))
    chosen = arr[...].reshape(SLOTS, width)
    gram[:width, :] = lax.dot_general(chosen, chosen, contract, preferred_element_type=F32) / ladder
    for e in range(1, DEPTH):
        spread(2, e)
    for e in range(1, DEPTH):
        spread(3, e)
    arr_copy.wait_recv()
    chosen_o = arr_o[...].reshape(SLOTS, width)
    gram[width:, :] = lax.dot_general(chosen_o, chosen, contract, preferred_element_type=F32) / ladder
    acc[...] += jnp.dot(amp[:, :unit], done(0), preferred_element_type=F32)
    acc[...] += jnp.dot(amp[:, unit:], done(1), preferred_element_type=F32)
    acc[...] += jnp.dot(other[:, :unit], done(2), preferred_element_type=F32)
    last[...] = done(3)
    for c in started:
        c.wait_send()


def finish_kernel(other, acc, last, out, held, sem):
    count, width = acc.shape
    unit = last.shape[0]
    tile = 512
    copies = []
    for t in range(count // tile):
        at = slice(t * tile, (t + 1) * tile)
        held[at, :] = (
            acc[at, :] + jnp.dot(other[at, width - unit :], last[...], preferred_element_type=F32)
        ).astype(BF16)
        c = pltpu.make_async_copy(held.at[pl.ds(t * tile, tile)], out.at[pl.ds(t * tile, tile)], sem.at[t])
        c.start()
        copies.append(c)
    for c in copies:
        c.wait()


def fused(amplitudes, cycle_ints, int_rows, row_dest, vir_energy, occ_energy):
    count, width = amplitudes.shape
    groups = DEPTH * PLANE
    unit = 2 * width // UNITS
    block = unit // PLANE
    dma = pltpu.SemaphoreType.DMA
    vmem = pl.BlockSpec(memory_space=pltpu.VMEM)
    other, acc, last = pl.pallas_call(
        kernel,
        out_shape=(
            pltpu.VMEM((count, width), BF16),
            pltpu.VMEM((count, width), F32),
            pltpu.VMEM((unit, width), BF16),
        ),
        in_specs=[pl.BlockSpec(memory_space=pltpu.HBM)] * 6,
        out_specs=[vmem] * 3,
        scratch_shapes=[
            pltpu.VMEM((count, width), BF16),
            pltpu.VMEM((count, width), BF16),
            pltpu.VMEM(int_rows.shape, BF16),
            pltpu.VMEM(row_dest.shape[::-1], jnp.int32),
            pltpu.VMEM((1, width), F32),
            pltpu.VMEM((count // 128, 128), F32),
            pltpu.VMEM((UNITS, unit, width), BF16),
            pltpu.VMEM((UNITS, 2, block, width), BF16),
            pltpu.VMEM((UNITS, block, width), BF16),
            pltpu.VMEM((UNITS, block, width), BF16),
            pltpu.VMEM((UNITS, DEPTH - 1, block // DEPTH, width), BF16),
            pltpu.VMEM((2 * width, width), BF16),
            pltpu.VMEM((DEPTH, PLANE, SLOTS // groups, width), BF16),
            pltpu.VMEM((DEPTH, PLANE, SLOTS // groups, width), BF16),
            pltpu.VMEM((DEPTH, PLANE, SLOTS // groups, width), BF16),
            pltpu.VMEM((DEPTH, PLANE, SLOTS // groups, width), BF16),
            pltpu.VMEM((2 * width, width), F32),
            pltpu.SemaphoreType.REGULAR,
            pltpu.SemaphoreType.REGULAR,
            pltpu.SemaphoreType.REGULAR((2,)),
            dma((7,)),
            dma((2, 2)),
            dma((2, 2, 3)),
            dma((2, 1)),
            dma((2, UNITS, 3)),
            dma((2, UNITS, DEPTH - 1)),
            dma((2, UNITS, DEPTH - 1)),
            dma((2, UNITS, DEPTH, PLANE - 1)),
        ],
        compiler_params=pltpu.CompilerParams(
            collective_id=0, has_side_effects=True, vmem_limit_bytes=56 * 2**20
        ),
    )(
        amplitudes, cycle_ints, int_rows, row_dest.T,
        vir_energy.reshape(1, width), occ_energy.reshape(count // 128, 128),
    )
    return pl.pallas_call(
        finish_kernel,
        out_shape=jax.ShapeDtypeStruct((count, width), BF16),
        in_specs=[vmem] * 3,
        out_specs=pl.BlockSpec(memory_space=pltpu.HBM),
        scratch_shapes=[pltpu.VMEM((count, width), BF16), dma((count // 512,))],
        compiler_params=pltpu.CompilerParams(vmem_limit_bytes=24 * 2**20),
    )(other, acc, last)


def solution(mesh):
    fits = mesh.shape["pair"] == DEPTH * PLANE and mesh.shape["vir"] == 2
    return jax.shard_map(
        fused if fits else body,
        mesh=mesh,
        in_specs=(
            P("pair", "vir"),
            P("pair", "vir"),
            P("pair", "vir"),
            P("pair", None),
            P("vir"),
            P("pair"),
        ),
        out_specs=P("pair", "vir"),
        check_vma=False,
    )
```

```python
import math

import jax
import jax.numpy as jnp
from jax import lax
from jax.experimental import pallas as pl
from jax.experimental.pallas import tpu as pltpu
from jax.sharding import PartitionSpec as P

SLOTS = 256


def dispatch(int_rows, row_dest, groups, capacity):
    rows = int_rows.shape[0]
    group = jnp.arange(groups, dtype=jnp.int32)
    member = jnp.any(row_dest[None, :, :] == group[:, None, None], axis=2)
    before = jnp.arange(rows)[:, None] < jnp.arange(rows)[None, :]
    rank = jnp.dot(
        member.astype(jnp.bfloat16), before.astype(jnp.bfloat16), preferred_element_type=jnp.float32
    ).astype(jnp.int32)
    slot = jnp.arange(capacity, dtype=jnp.int32)
    select = member[:, None, :] & (rank[:, None, :] == slot[None, :, None])
    select = select.reshape(groups * capacity, rows).astype(int_rows.dtype)
    return jnp.dot(select, int_rows, preferred_element_type=jnp.float32).astype(int_rows.dtype)


def body(amplitudes, cycle_ints, int_rows, row_dest, vir_energy, occ_energy):
    groups = lax.axis_size("pair")
    row_count, local_width = amplitudes.shape
    full_width = local_width * lax.axis_size("vir")
    capacity = SLOTS // groups
    gathered = lax.all_gather(amplitudes, "vir", axis=1, tiled=True)
    cross_part = lax.dot_general(
        gathered, cycle_ints, (((0,), (0,)), ((), ())), preferred_element_type=jnp.float32
    )
    scale_cycle = math.sqrt(row_count * groups * full_width)
    cross_half = lax.psum((cross_part / scale_cycle).astype(jnp.bfloat16), "pair")
    outgoing = dispatch(int_rows, row_dest, groups, capacity)
    arrived = lax.all_to_all(
        outgoing.reshape(groups, capacity, local_width),
        "pair",
        split_axis=0,
        concat_axis=0,
        tiled=True,
    ).reshape(groups * capacity, local_width)
    chosen = lax.all_gather(arrived, "vir", axis=1, tiled=True)
    coefficient = lax.dot_general(
        gathered, chosen, (((1,), (1,)), ((), ())), preferred_element_type=jnp.float32
    ) / math.sqrt(full_width)
    ladder = jnp.dot(
        coefficient.astype(jnp.bfloat16), arrived, preferred_element_type=jnp.float32
    ) / math.sqrt(SLOTS)
    energy = (vir_energy[None, :] - occ_energy[:, None]) * amplitudes.astype(jnp.float32)
    cycle_term = jnp.dot(gathered, cross_half, preferred_element_type=jnp.float32)
    return (cycle_term + ladder + energy).astype(jnp.bfloat16)


DEPTH, PLANE, UNITS = 4, 4, 4
F32, BF16 = jnp.float32, jnp.bfloat16
MESH = pl.DeviceIdType.MESH


def rows_at(start, size):
    return pl.ds(pl.multiple_of(start, size), size)


def kernel(
    amp_hbm, cyc_hbm, rows_hbm, dest_hbm, vir_hbm, occ_hbm, other, acc, last,
    amp, cyc, rows, dest, vir_e, occ_e, part, first_in, second_in, zsum, z_in, full,
    outgoing, mid, arr, arr_o, gram,
    core_sem, near_sem, hop_sem, load_sem, amp_sem, route_sem, arr_sem, sum_sem, z_sem, gz_sem, spread_sem,
):
    groups = DEPTH * PLANE
    me, v = lax.axis_index("pair"), lax.axis_index("vir")
    z, y, x = me // PLANE, me % PLANE // 2, me % 2
    by_x, by_y, by_xy = me + 1 - 2 * x, me + 2 - 4 * y, z * PLANE + 3 - me % PLANE
    count, width = amp.shape
    full_width = 2 * width
    capacity = SLOTS // groups
    unit = full_width // UNITS
    block = unit // PLANE
    piece = block // DEPTH

    left, right = pl.ds(0, unit), pl.ds(unit, unit)
    loads = [
        pltpu.make_async_copy(src, dst, load_sem.at[i])
        for i, (src, dst) in enumerate(
            (
                (cyc_hbm, cyc), (amp_hbm.at[:, left], amp.at[:, left]), (amp_hbm.at[:, right], amp.at[:, right]),
                (dest_hbm, dest), (rows_hbm, rows), (vir_hbm, vir_e), (occ_hbm, occ_e),
            )
        )
    ]
    for c in loads:
        c.start()

    def signal(sem, to, core):
        pl.semaphore_signal(sem, inc=1, device_id=(to, core), device_id_type=MESH)

    def signal_depth(sem, core):
        @pl.when(z > 0)
        def _():
            signal(sem, me - PLANE, core)

        @pl.when(z < DEPTH - 1)
        def _():
            signal(sem, me + PLANE, core)

    barrier = pltpu.get_barrier_semaphore()

    @pl.when(v == 1)
    def _():
        signal(barrier, me, 0)

    signal(barrier, by_x, 1)
    signal(barrier, by_y, 1)
    signal_depth(barrier, 1)
    ends = jnp.where(z > 0, 1, 0) + jnp.where(z < DEPTH - 1, 1, 0)

    @pl.when(v == 0)
    def _():
        pl.semaphore_wait(barrier, 1)
        signal(core_sem, me, 1)

    @pl.when(v == 1)
    def _():
        pl.semaphore_wait(core_sem, 1)

    started = []

    def copy(src, dst, sem, index, device):
        c = pltpu.make_async_remote_copy(
            src_ref=src,
            dst_ref=dst,
            send_sem=sem.at[(0, *index)],
            recv_sem=sem.at[(1, *index)],
            device_id=device,
            device_id_type=MESH,
        )
        c.start()
        started.append(c)
        return c

    def dispatch():
        group = lax.broadcasted_iota(jnp.int32, (SLOTS, rows.shape[0]), 0) // capacity
        slot = lax.broadcasted_iota(jnp.int32, (SLOTS, rows.shape[0]), 0) % capacity
        member = group == dest[0:1, :]
        for k in range(1, dest.shape[0]):
            member = member | (group == dest[k : k + 1, :])
        tri = (rows.shape[0], rows.shape[0])
        before = lax.broadcasted_iota(jnp.int32, tri, 0) < lax.broadcasted_iota(jnp.int32, tri, 1)
        rank = jnp.dot(
            jnp.where(member, 1.0, 0.0).astype(BF16),
            jnp.where(before, 1.0, 0.0).astype(BF16),
            preferred_element_type=F32,
        )
        select = jnp.where(member & (rank == slot.astype(F32)), 1.0, 0.0).astype(BF16)
        outgoing[...] = jnp.dot(select, rows[...], preferred_element_type=F32).astype(BF16).reshape(outgoing.shape)

    routed = []

    def route_depth(i):
        to = (z + 1 - 2 * (z % 2), (z + 2) % DEPTH, DEPTH - 1 - z)[i]
        routed.append(
            copy(outgoing.at[to], mid.at[z], route_sem, (0, i), (to * PLANE + me % PLANE, v))
        )

    def route_plane():
        for c in routed:
            c.wait_recv()
        q = me % PLANE
        mid[z] = outgoing[z]
        arr[:, q] = mid[:, q]
        return [
            copy(mid.at[:, to % PLANE], arr.at[:, q], route_sem, (1, i), (to, v))
            for i, to in enumerate((by_x, by_y, by_xy))
        ]

    def cross(u):
        src = amp if u < UNITS // 2 else other
        at = u % (UNITS // 2) * unit
        part[u] = lax.dot_general(
            src[:, at : at + unit], cyc[...], (((0,), (0,)), ((), ())), preferred_element_type=F32
        ).astype(BF16)

    def axes(u):
        return (x, y, by_x, by_y) if u % 2 == 0 else (y, x, by_y, by_x)

    def quarter(a, b):
        return rows_at((a * 2 + b) * block, block)

    sums = {}

    def sum_first(u):
        a, b, by_a, by_b = axes(u)
        sums[u, 2] = copy(
            part.at[u, quarter(a, 1 - b)], second_in.at[u], sum_sem, (u, 2), (by_b, v)
        )
        sums[u, 1] = copy(
            part.at[u, quarter(1 - a, b)], first_in.at[u, 1], sum_sem, (u, 1), (by_a, v)
        )

    def sum_across(u):
        a, b, by_a, by_b = axes(u)
        sums[u, 0] = copy(
            part.at[u, quarter(1 - a, 1 - b)], first_in.at[u, 0], sum_sem, (u, 0), (by_xy, v)
        )

    def sum_third(u):
        a, b, by_a, by_b = axes(u)
        total = part[u, quarter(a, b), :].astype(F32)
        sums[u, 1].wait_recv()
        total += first_in[u, 1].astype(F32)
        sums[u, 0].wait_recv()
        total += first_in[u, 0].astype(F32)
        sums[u, 2].wait_recv()
        zsum[u] = (total + second_in[u].astype(F32)).astype(BF16)
        for e in range(1, DEPTH):
            to = (z + e) % DEPTH
            sums[u, 2 + e] = copy(
                zsum.at[u, rows_at(to * piece, piece)], z_in.at[u, e - 1],
                z_sem, (u, e - 1), (to * PLANE + me % PLANE, v),
            )

    scale = math.sqrt(count * groups * full_width)
    spreads, planes = {}, {}

    def finish(u):
        a, b, by_a, by_b = axes(u)
        total = zsum[u, rows_at(z * piece, piece), :].astype(F32)
        for e in range(1, DEPTH):
            sums[u, 2 + e].wait_recv()
            total += z_in[u, e - 1].astype(F32)
        at = rows_at(((u * 2 + a) * 2 + b) * block + z * piece, piece)
        full[at, :] = (total / scale).astype(BF16)
        for e in range(1, DEPTH):
            spreads[u, e] = copy(
                full.at[at], full.at[at], gz_sem, (u, e - 1),
                ((z + e) % DEPTH * PLANE + me % PLANE, v),
            )

    def spread(u, e):
        a, b, by_a, by_b = axes(u)
        if e:
            spreads[u, e].wait_recv()
        at = rows_at(((u * 2 + a) * 2 + b) * block + (z - e + DEPTH) % DEPTH * piece, piece)
        for i, to in enumerate((by_xy, by_b, by_a)):
            planes[u, e, i] = copy(full.at[at], full.at[at], spread_sem, (u, e, i), (to, v))

    def done(u):
        for e in range(DEPTH):
            for i in range(PLANE - 1):
                planes[u, e, i].wait_recv()
        at = slice(u * unit, (u + 1) * unit)
        return (full[at, :].astype(F32) + gram[at, :]).astype(BF16)

    def energy():
        for t in range(count // 128):
            at = slice(t * 128, (t + 1) * 128)
            line = jnp.broadcast_to(occ_e[t : t + 1, :], (128, 128)).T
            for b in range(width // 128):
                cols = slice(b * 128, (b + 1) * 128)
                acc[at, cols] = (vir_e[:, cols] - line) * amp[at, cols].astype(F32)

    amp_copies = []
    for i, at in enumerate((left, right)):
        amp_copies.append(copy(amp_hbm.at[:, at], other.at[:, at], amp_sem, (i,), (me, 1 - v)))
    loads[0].wait()
    loads[1].wait()
    cross(0)

    @pl.when(v == 1)
    def _():
        pl.semaphore_wait(barrier, 2 * (2 + ends))
        signal(near_sem, me, 0)

    @pl.when(v == 0)
    def _():
        pl.semaphore_wait(near_sem, 1)

    signal(hop_sem.at[0], by_x, v)
    signal(hop_sem.at[0], by_y, v)
    signal_depth(hop_sem.at[0], v)
    sum_first(0)
    loads[2].wait()
    cross(1)
    sum_first(1)
    pl.semaphore_wait(hop_sem.at[0], 2 + ends)
    signal_depth(hop_sem.at[1], v)
    sum_across(0)
    sum_across(1)
    for c in loads[3:]:
        c.wait()
    dispatch()
    route_depth(0)
    route_depth(1)
    amp_copies[0].wait_recv()
    cross(2)
    sum_first(2)
    sum_across(2)
    pl.semaphore_wait(hop_sem.at[1], ends)
    route_depth(2)
    amp_copies[1].wait_recv()
    cross(3)
    sum_first(3)
    sum_across(3)
    sum_third(0)
    routed = route_plane()
    sum_third(1)
    energy()
    sum_third(2)
    finish(0)
    spread(0, 0)
    finish(1)
    spread(1, 0)
    sum_third(3)
    finish(2)
    spread(2, 0)
    for e in range(1, DEPTH):
        spread(0, e)
    for e in range(1, DEPTH):
        spread(1, e)
    finish(3)
    spread(3, 0)
    for c in routed:
        c.wait_recv()
    arr_copy = copy(arr, arr_o, arr_sem, (0,), (me, 1 - v))
    ladder = math.sqrt(full_width) * math.sqrt(SLOTS)
    contract = (((0,), (0,)), ((), ()))
    chosen = arr[...].reshape(SLOTS, width)
    gram[:width, :] = lax.dot_general(chosen, chosen, contract, preferred_element_type=F32) / ladder
    for e in range(1, DEPTH):
        spread(2, e)
    for e in range(1, DEPTH):
        spread(3, e)
    arr_copy.wait_recv()
    chosen_o = arr_o[...].reshape(SLOTS, width)
    gram[width:, :] = lax.dot_general(chosen_o, chosen, contract, preferred_element_type=F32) / ladder
    acc[...] += jnp.dot(amp[:, :unit], done(0), preferred_element_type=F32)
    acc[...] += jnp.dot(amp[:, unit:], done(1), preferred_element_type=F32)
    acc[...] += jnp.dot(other[:, :unit], done(2), preferred_element_type=F32)
    last[...] = done(3)
    for c in started:
        c.wait_send()


def finish_kernel(other, acc, last, out, held, sem):
    count, width = acc.shape
    unit = last.shape[0]
    tile = 256
    copies = []
    for t in range(count // tile):
        at = slice(t * tile, (t + 1) * tile)
        held[at, :] = (
            acc[at, :] + jnp.dot(other[at, width - unit :], last[...], preferred_element_type=F32)
        ).astype(BF16)
        c = pltpu.make_async_copy(held.at[pl.ds(t * tile, tile)], out.at[pl.ds(t * tile, tile)], sem.at[t])
        c.start()
        copies.append(c)
    for c in copies:
        c.wait()


def fused(amplitudes, cycle_ints, int_rows, row_dest, vir_energy, occ_energy):
    count, width = amplitudes.shape
    groups = DEPTH * PLANE
    unit = 2 * width // UNITS
    block = unit // PLANE
    dma = pltpu.SemaphoreType.DMA
    vmem = pl.BlockSpec(memory_space=pltpu.VMEM)
    other, acc, last = pl.pallas_call(
        kernel,
        out_shape=(
            pltpu.VMEM((count, width), BF16),
            pltpu.VMEM((count, width), F32),
            pltpu.VMEM((unit, width), BF16),
        ),
        in_specs=[pl.BlockSpec(memory_space=pltpu.HBM)] * 6,
        out_specs=[vmem] * 3,
        scratch_shapes=[
            pltpu.VMEM((count, width), BF16),
            pltpu.VMEM((count, width), BF16),
            pltpu.VMEM(int_rows.shape, BF16),
            pltpu.VMEM(row_dest.shape[::-1], jnp.int32),
            pltpu.VMEM((1, width), F32),
            pltpu.VMEM((count // 128, 128), F32),
            pltpu.VMEM((UNITS, unit, width), BF16),
            pltpu.VMEM((UNITS, 2, block, width), BF16),
            pltpu.VMEM((UNITS, block, width), BF16),
            pltpu.VMEM((UNITS, block, width), BF16),
            pltpu.VMEM((UNITS, DEPTH - 1, block // DEPTH, width), BF16),
            pltpu.VMEM((2 * width, width), BF16),
            pltpu.VMEM((DEPTH, PLANE, SLOTS // groups, width), BF16),
            pltpu.VMEM((DEPTH, PLANE, SLOTS // groups, width), BF16),
            pltpu.VMEM((DEPTH, PLANE, SLOTS // groups, width), BF16),
            pltpu.VMEM((DEPTH, PLANE, SLOTS // groups, width), BF16),
            pltpu.VMEM((2 * width, width), F32),
            pltpu.SemaphoreType.REGULAR,
            pltpu.SemaphoreType.REGULAR,
            pltpu.SemaphoreType.REGULAR((2,)),
            dma((7,)),
            dma((2, 2)),
            dma((2, 2, 3)),
            dma((2, 1)),
            dma((2, UNITS, 3)),
            dma((2, UNITS, DEPTH - 1)),
            dma((2, UNITS, DEPTH - 1)),
            dma((2, UNITS, DEPTH, PLANE - 1)),
        ],
        compiler_params=pltpu.CompilerParams(
            collective_id=0, has_side_effects=True, vmem_limit_bytes=56 * 2**20
        ),
    )(
        amplitudes, cycle_ints, int_rows, row_dest.T,
        vir_energy.reshape(1, width), occ_energy.reshape(count // 128, 128),
    )
    return pl.pallas_call(
        finish_kernel,
        out_shape=jax.ShapeDtypeStruct((count, width), BF16),
        in_specs=[vmem] * 3,
        out_specs=pl.BlockSpec(memory_space=pltpu.HBM),
        scratch_shapes=[pltpu.VMEM((count, width), BF16), dma((count // 256,))],
        compiler_params=pltpu.CompilerParams(vmem_limit_bytes=24 * 2**20),
    )(other, acc, last)


def solution(mesh):
    fits = mesh.shape["pair"] == DEPTH * PLANE and mesh.shape["vir"] == 2
    return jax.shard_map(
        fused if fits else body,
        mesh=mesh,
        in_specs=(
            P("pair", "vir"),
            P("pair", "vir"),
            P("pair", "vir"),
            P("pair", None),
            P("vir"),
            P("pair"),
        ),
        out_specs=P("pair", "vir"),
        check_vma=False,
    )
```
